32 devices in a mesh: dp: 2 (over x), layer: 4 (over y, core), feat: 4 (over z).
Axes of the slice: x: 2, y: 2, z: 4, core: 2. Of those that a mesh axis runs over, the one named last changes fastest.
Arguments:
- resid: bfloat16 [4, 1024, 2304], P('layer', 'dp'), may hold values from -6 to 6
- enc_weight: bfloat16 [4, 2304, 2048], P('layer', None, 'feat'), may hold values from -0.125 to 0.125
- enc_bias: float32 [4, 2048], P('layer', 'feat'), may hold values from -3 to 3
- dec_weight: bfloat16 [4, 4, 2048, 2304], P('layer', None, 'feat', 'dp'), may hold values from -0.1875 to 0.1875
- dec_bias: float32 [4, 2304], P('layer', ('dp', 'feat')), may hold values from -3 to 3
- lengths: int32 [8], P('dp'), may hold values from 32 to 128, as said below
Outputs:
- recon: bfloat16 [4, 1024, 2304], P('layer', None, ('dp', 'feat'))
The draws below stay inside these ranges and needn't reach their ends.
Inputs may be any that keep to these rules, and one draw needn't show every extreme that they name: `lengths`: the first sequence has length 128.
All inputs are finite; a program needn't handle non-finite values.
Results may differ from the reference program's by a relative error of at most 0.0047.
Values may be sent and summed in bfloat16 or wider, within the bound.
A program may use at most 64 MiB of HBM per device.

```python
import jax
import jax.numpy as jnp

D = 2304
FEATS = 2048
LAYERS = 4
SEQ = 128
ROWS = 1024
NSEQ = 8


def draw_lengths(key, part):
    lowest = max(1, SEQ // 4)
    drawn = jax.random.randint(key, (NSEQ,), lowest, SEQ + 1).astype(jnp.int32)
    return drawn.at[0].set(SEQ)


def spiked(entries, key, source, target, parts, factor):
    owner, partner = [(jnp.arange(entries.shape[dim]) // (entries.shape[dim] // parts)).reshape([-1 if axis == dim else 1 for axis in range(entries.ndim)]) for dim in (source, target)]
    chosen = jax.random.permutation(key, parts)[partner]
    strong = (owner == chosen) | (owner == (partner + parts // 2) % parts)
    return jnp.where(strong, factor * entries, entries)


def steps_of(rng, shape, shards, smallest, largest):
    level = 1.0
    for axis_at, parts in shards:
        heights = jax.random.uniform(jax.random.fold_in(jax.random.fold_in(rng, 6), axis_at), (parts,), jnp.float32, smallest / len(shards), largest / len(shards))
        level = level * jnp.repeat(jnp.exp(heights), shape[axis_at] // parts).reshape((-1,) + (1,) * (len(shape) - 1 - axis_at))
    return level


def bell_draw(stream_key, dims, deviation, reach, shards=(), held_as=jnp.bfloat16):
    loudness = steps_of(stream_key, dims, shards, -0.22, 0.18) if shards else 1.0
    entries = jax.random.normal(stream_key, dims, jnp.float32) * deviation * loudness
    return jnp.minimum(jnp.maximum(entries, -reach), reach).astype(held_as)


def noise_with(key, dims, scale, reach, shards, heavy, dtype=jnp.bfloat16):
    result = scale * jax.random.normal(key, dims, jnp.float32)
    if shards:
        result = result * steps_of(key, dims, shards, -0.22, 0.18)
    return jnp.clip(spiked(result, jax.random.fold_in(key, 3), *heavy), -reach, reach).astype(dtype)


def setup_inputs(seed: int = 0) -> dict:
    arg_keys = jax.random.split(jax.random.key(seed), 7)
    return {
        "resid": bell_draw(arg_keys[0], (LAYERS, ROWS, D), 1.0, 6.0, ((0, 4), (1, 2))),
        "enc_weight": bell_draw(arg_keys[1], (LAYERS, D, FEATS), D ** -0.5, 0.125, ((0, 4), (2, 4))),
        "enc_bias": bell_draw(arg_keys[2], (LAYERS, FEATS), 0.5, 3.0, ((0, 4), (1, 4)), jnp.float32),
        "dec_weight": noise_with(arg_keys[3], (LAYERS, LAYERS, FEATS, D), FEATS ** -0.5, 0.1875, ((0, 4), (2, 4), (3, 2)), (2, 3, 4, 2.0)),
        "dec_bias": bell_draw(arg_keys[4], (LAYERS, D), 0.5, 3.0, ((0, 4), (1, 8)), jnp.float32),
        "lengths": draw_lengths(jax.random.fold_in(arg_keys[6], 71), 0),
    }


def reference(resid, enc_weight, enc_bias, dec_weight, dec_bias, lengths):
    valid = (jnp.arange(SEQ)[None, :] < lengths[:, None]).reshape(-1).astype(jnp.float32)
    acts = []
    for source in range(LAYERS):
        pre = jnp.dot(resid[source], enc_weight[source], preferred_element_type=jnp.float32) + enc_bias[source]
        acts.append((jax.nn.relu(pre) * valid[:, None]).astype(jnp.bfloat16))
    outputs = []
    for target in range(LAYERS):
        total = jnp.zeros((resid.shape[1], resid.shape[2]), jnp.float32)
        for source in range(target + 1):
            total = total + jnp.dot(acts[source], dec_weight[target, source], preferred_element_type=jnp.float32)
        outputs.append((total + dec_bias[target]).astype(jnp.bfloat16))
    return jnp.stack(outputs)
```

```python
import functools

import jax
import jax.numpy as jnp
from jax import lax
from jax.experimental import pallas as pl
from jax.experimental.pallas import tpu as pltpu
from jax.sharding import PartitionSpec as P

SEQ = 128
LANES = 128
MESH = pl.DeviceIdType.MESH


def passed_along(array, axis, by):
    size = lax.axis_size(axis)
    pairs = [(i, i + by) for i in range(size) if 0 <= i + by < size]
    return lax.ppermute(array, axis, pairs)


def with_collectives(resid, enc_weight, enc_bias, dec_weight, dec_bias, lengths):
    valid = (jnp.arange(SEQ)[None, :] < lengths[:, None]).reshape(-1).astype(jnp.float32)
    pre = jnp.dot(resid[0], enc_weight[0], preferred_element_type=jnp.float32) + enc_bias[0]
    acts = (jax.nn.relu(pre) * valid[:, None]).astype(jnp.bfloat16)
    target = lax.axis_index("layer")
    decoders = dec_weight[0]
    all_rows = lax.all_gather(acts, "dp", axis=0, tiled=True)
    initial = jnp.zeros((all_rows.shape[0], decoders.shape[2]), jnp.float32)
    pieces = [(all_rows, target)]
    current = all_rows
    for step in range(1, lax.axis_size("layer")):
        current = passed_along(current, "layer", 1)
        pieces.append((current, target - step))
    total = initial
    for block, source in pieces:

        def apply_dec(carry):
            matrix = lax.dynamic_index_in_dim(decoders, jnp.maximum(source, 0), 0, keepdims=False)
            return carry + jnp.dot(block, matrix, preferred_element_type=jnp.float32)

        total = lax.cond((source >= 0) & (source <= target), apply_dec, lambda carry: carry, total)
    summed = lax.psum_scatter(total, "feat", scatter_dimension=1, tiled=True)
    return (summed + dec_bias[0][None, :]).astype(jnp.bfloat16)[None]


def kernel(
    n_feat, n_layer, blocks, rows, main, rem,
    lengths_ref, resid_hbm, encw_hbm, encb_ref, decw_hbm, decb_ref,
    out_ref,
    resid, encw, decw, acts, acc, part, sbuf, from_low, from_high,
    load_sem, dec_sem, acts_sem, dp_send, sib_send, far_send, relay_send, z_send, low_sem, high_sem,
):
    dp, layer, z = lax.axis_index("dp"), lax.axis_index("layer"), lax.axis_index("feat")
    chunk = main + rem
    packs = main // rem
    tall = rows // packs
    half = n_layer // 2
    sibling = layer + 1 - 2 * (layer % 2)
    own = blocks // 2

    loads = [pltpu.make_async_copy(encw_hbm, encw, load_sem.at[0])]
    for b in range(own):
        span = pl.ds(b * rows, rows)
        loads.append(pltpu.make_async_copy(resid_hbm.at[span], resid.at[span], load_sem.at[1 + b]))
    for load in loads:
        load.start()
    dec_loads = [pltpu.make_async_copy(decw_hbm.at[s], decw.at[s], dec_sem.at[s]) for s in range(n_layer)]
    for load in dec_loads:
        load.start()

    barrier = pltpu.get_barrier_semaphore()
    partner = (layer + half) % n_layer
    for where in ({"dp": 1 - dp}, {"layer": sibling}, {"layer": partner}):
        pl.semaphore_signal(barrier, inc=1, device_id=where, device_id_type=MESH)

    @pl.when(z > 0)
    def _():
        pl.semaphore_signal(barrier, inc=1, device_id={"feat": z - 1}, device_id_type=MESH)

    @pl.when(z < n_feat - 1)
    def _():
        pl.semaphore_signal(barrier, inc=1, device_id={"feat": z + 1}, device_id_type=MESH)

    ends = jnp.where(z == 0, 1, 0) + jnp.where(z == n_feat - 1, 1, 0)
    pl.semaphore_wait(barrier, 5 - ends)

    def block_of(i):
        return (dp if i < own else 1 - dp) * own + i % own

    def sent(source, i, sems, where):
        block = block_of(i)
        return pltpu.make_async_remote_copy(
            src_ref=acts.at[source, block],
            dst_ref=acts.at[source, block],
            send_sem=sems.at[i],
            recv_sem=acts_sem.at[source, block],
            device_id=where,
            device_id_type=MESH,
        )

    def dp_copy(i):
        return sent(layer, i, dp_send, {"dp": 1 - dp})

    def sib_copy(i):
        return sent(layer, i, sib_send, {"layer": sibling})

    def far_copy(i):
        return sent(layer, i, far_send, {"layer": partner})

    def relay_copy(i):
        return sent(partner, i, relay_send, {"layer": sibling})

    def arrived(source, i):
        sent(source, i, dp_send, {"dp": 1 - dp}).wait_recv()

    def spread(i):
        @pl.when(layer < half)
        def _():
            far_copy(i).start()

        @pl.when(layer % 2 == 0)
        def _():
            sib_copy(i).start()

    def encode(i):
        pre = jnp.dot(resid[i * rows : (i + 1) * rows], encw[...], preferred_element_type=jnp.float32)
        pre = jnp.maximum(pre + encb_ref[...], 0.0)
        for k in range(rows // SEQ):
            length = lengths_ref[i * (rows // SEQ) + k]
            piece = pre[k * SEQ : (k + 1) * SEQ]
            position = lax.broadcasted_iota(jnp.int32, piece.shape, 0)
            piece = jnp.where(position < length, piece, 0.0)
            acts[layer, block_of(i), pl.ds(k * SEQ, SEQ), :] = piece.astype(jnp.bfloat16)
        dp_copy(i).start()
        spread(i)

    def take(i):
        arrived(layer, i)
        spread(i)

    def relay(i):
        @pl.when(layer >= half)
        def _():
            arrived(layer - half, i)
            relay_copy(i).start()

    def z_copy(i, j, up):
        landing, sems = (from_low, low_sem) if up else (from_high, high_sem)
        return pltpu.make_async_remote_copy(
            src_ref=sbuf.at[i, j],
            dst_ref=landing.at[i, j],
            send_sem=z_send.at[i, j],
            recv_sem=sems.at[i, j],
            device_id={"feat": z + 1 if up else z - 1},
            device_id_type=MESH,
        )

    def decode(i):
        block = block_of(i)
        acc[...] = jnp.dot(acts[layer, block], decw[layer], preferred_element_type=jnp.float32)
        for s in range(n_layer - 1):

            @pl.when(s < layer)
            def _():
                @pl.when(s + half != layer)
                def _():
                    arrived(s, i)

                acc[...] += jnp.dot(acts[s, block], decw[s], preferred_element_type=jnp.float32)

        for j in range(n_feat):
            first = j * chunk
            part[i, j, 0:rows, :] = acc[:, first : first + main]
            tail = acc[:, first + main : first + chunk]
            part[i, j, rows : rows + tall, :] = jnp.concatenate(
                [tail[k * tall : (k + 1) * tall] for k in range(packs)], axis=1
            )

        @pl.when(z == 0)
        def _():
            for j in reversed(range(1, n_feat)):
                sbuf[i, j] = part[i, j].astype(jnp.bfloat16)
                z_copy(i, j, True).start()

        @pl.when(z == n_feat - 1)
        def _():
            for j in range(n_feat - 1):
                sbuf[i, j] = part[i, j].astype(jnp.bfloat16)
                z_copy(i, j, False).start()

    def forward(i, j, up):
        z_copy(i, j, up).wait_recv()
        landing = from_low if up else from_high
        sbuf[i, j] = (part[i, j] + landing[i, j].astype(jnp.float32)).astype(jnp.bfloat16)
        z_copy(i, j, up).start()

    def finish(i):
        for place in range(1, n_feat - 1):

            @pl.when(z == place)
            def _():
                ups = [(j, True) for j in reversed(range(place + 1, n_feat))]
                downs = [(j, False) for j in range(place)]
                order = ups + downs if len(ups) >= len(downs) else downs + ups
                for j, up in order:
                    forward(i, j, up)

        @pl.when(z > 0)
        def _():
            z_copy(i, z, True).wait_recv()
            part[i, z] += from_low[i, z].astype(jnp.float32)

        @pl.when(z < n_feat - 1)
        def _():
            z_copy(i, z, False).wait_recv()
            part[i, z] += from_high[i, z].astype(jnp.float32)

        start = block_of(i) * rows
        bias = decb_ref[...]
        out_ref[pl.ds(start, rows), 0:main] = (part[i, z, 0:rows, :] + bias[:, 0:main]).astype(jnp.bfloat16)
        tail = part[i, z, rows : rows + tall, :]
        tail = jnp.concatenate([tail[:, k * rem : (k + 1) * rem] for k in range(packs)], axis=0)
        out_ref[pl.ds(start, rows), main:chunk] = (tail + bias[:, main:chunk]).astype(jnp.bfloat16)

    loads[0].wait()
    for i in range(own):
        loads[1 + i].wait()
        encode(i)
    relay(0)
    for load in dec_loads:
        load.wait()
    decode(0)
    for i in range(1, blocks):
        if i == 1:
            for later in range(own, blocks):
                relay(1) if later == own else None
                take(later)
        else:
            relay(i)
        decode(i)
        finish(i - 1)
    finish(blocks - 1)

    for i in range(blocks):
        if i < own:
            dp_copy(i).wait_send()

        @pl.when(layer < half)
        def _():
            far_copy(i).wait_send()

        @pl.when(layer % 2 == 0)
        def _():
            sib_copy(i).wait_send()

        @pl.when(layer >= half)
        def _():
            relay_copy(i).wait_send()

        for j in range(n_feat):

            @pl.when(z != j)
            def _():
                z_copy(i, j, True).wait_send()


def with_kernel(n_feat, n_layer, resid, enc_weight, enc_bias, dec_weight, dec_bias, lengths):
    _, own_rows, width = resid.shape
    feats = enc_weight.shape[2]
    columns = dec_weight.shape[3]
    chunk = columns // n_feat
    main = chunk // LANES * LANES
    rem = chunk - main
    rows = own_rows // 2
    blocks = 4
    tall = rows // (main // rem)
    packed = (blocks, n_feat, rows + tall, main)
    anywhere = pl.BlockSpec(memory_space=pl.ANY)
    vmem = pl.BlockSpec(memory_space=pltpu.VMEM)
    dma = pltpu.SemaphoreType.DMA
    out = pl.pallas_call(
        functools.partial(kernel, n_feat, n_layer, blocks, rows, main, rem),
        out_shape=jax.ShapeDtypeStruct((2 * own_rows, chunk), jnp.bfloat16),
        in_specs=[pl.BlockSpec(memory_space=pltpu.SMEM), anywhere, anywhere, vmem, anywhere, vmem],
        out_specs=vmem,
        scratch_shapes=[
            pltpu.VMEM((own_rows, width), jnp.bfloat16),
            pltpu.VMEM((width, feats), jnp.bfloat16),
            pltpu.VMEM((n_layer, feats, columns), jnp.bfloat16),
            pltpu.VMEM((n_layer, blocks, rows, feats), jnp.bfloat16),
            pltpu.VMEM((rows, columns), jnp.float32),
            pltpu.VMEM(packed, jnp.float32),
            pltpu.VMEM(packed, jnp.bfloat16),
            pltpu.VMEM(packed, jnp.bfloat16),
            pltpu.VMEM(packed, jnp.bfloat16),
            dma((3,)),
            dma((n_layer,)),
            dma((n_layer, blocks)),
            dma((blocks,)),
            dma((blocks,)),
            dma((blocks,)),
            dma((blocks,)),
            dma((blocks, n_feat)),
            dma((blocks, n_feat)),
            dma((blocks, n_feat)),
        ],
        compiler_params=pltpu.CompilerParams(
            collective_id=0, has_side_effects=True, vmem_limit_bytes=56 * 2**20
        ),
    )(lengths, resid[0], enc_weight[0], enc_bias, dec_weight[0], dec_bias)
    return out[None]


def suits_kernel(sizes, resid, dec_weight):
    chunk = dec_weight.shape[3] // (sizes["dp"] * sizes["feat"])
    main, rem = chunk // LANES * LANES, chunk % LANES
    rows = resid.shape[1] // (2 * sizes["dp"])
    if sizes["dp"] != 2 or sizes["layer"] != 4 or sizes["feat"] < 2 or main == 0 or rem == 0:
        return False
    return main % rem == 0 and rows % SEQ == 0 and rows % (16 * (main // rem)) == 0


def solution(mesh):
    in_specs = (
        P("layer", "dp", None),
        P("layer", None, "feat"),
        P("layer", "feat"),
        P("layer", None, "feat", "dp"),
        P("layer", ("dp", "feat")),
        P("dp"),
    )
    out_specs = P("layer", None, ("dp", "feat"))
    sizes = dict(mesh.shape)

    def whole(resid, enc_weight, enc_bias, dec_weight, dec_bias, lengths):
        body = with_collectives
        if suits_kernel(sizes, resid, dec_weight):
            body = functools.partial(with_kernel, sizes["feat"], sizes["layer"])
        mapped = jax.shard_map(body, mesh=mesh, in_specs=in_specs, out_specs=out_specs, check_vma=False)
        return mapped(resid, enc_weight, enc_bias, dec_weight, dec_bias, lengths)

    return whole
```

```python
import functools

import jax
import jax.numpy as jnp
from jax import lax
from jax.experimental import pallas as pl
from jax.experimental.pallas import tpu as pltpu
from jax.sharding import PartitionSpec as P

SEQ = 128
LANES = 128
BLOCKS = 8
LAG = 3
MESH = pl.DeviceIdType.MESH


def passed_along(array, axis, by):
    size = lax.axis_size(axis)
    pairs = [(i, i + by) for i in range(size) if 0 <= i + by < size]
    return lax.ppermute(array, axis, pairs)


def with_collectives(resid, enc_weight, enc_bias, dec_weight, dec_bias, lengths):
    valid = (jnp.arange(SEQ)[None, :] < lengths[:, None]).reshape(-1).astype(jnp.float32)
    pre = jnp.dot(resid[0], enc_weight[0], preferred_element_type=jnp.float32) + enc_bias[0]
    acts = (jax.nn.relu(pre) * valid[:, None]).astype(jnp.bfloat16)
    target = lax.axis_index("layer")
    decoders = dec_weight[0]
    all_rows = lax.all_gather(acts, "dp", axis=0, tiled=True)
    initial = jnp.zeros((all_rows.shape[0], decoders.shape[2]), jnp.float32)
    pieces = [(all_rows, target)]
    current = all_rows
    for step in range(1, lax.axis_size("layer")):
        current = passed_along(current, "layer", 1)
        pieces.append((current, target - step))
    total = initial
    for block, source in pieces:

        def apply_dec(carry):
            matrix = lax.dynamic_index_in_dim(decoders, jnp.maximum(source, 0), 0, keepdims=False)
            return carry + jnp.dot(block, matrix, preferred_element_type=jnp.float32)

        total = lax.cond((source >= 0) & (source <= target), apply_dec, lambda carry: carry, total)
    summed = lax.psum_scatter(total, "feat", scatter_dimension=1, tiled=True)
    return (summed + dec_bias[0][None, :]).astype(jnp.bfloat16)[None]


def kernel(
    n_feat, n_layer, blocks, rows, main, rem,
    lengths_ref, resid_hbm, encw_hbm, encb_ref, decw_hbm, decb_ref,
    out_ref,
    resid, encw, decw, acts, acc, part, sbuf, from_low, from_high,
    load_sem, dec_sem, acts_sem, dp_send, sib_send, far_send, relay_send, z_send, low_sem, high_sem,
):
    dp, layer, z = lax.axis_index("dp"), lax.axis_index("layer"), lax.axis_index("feat")
    chunk = main + rem
    packs = main // rem
    tall = rows // packs
    half = n_layer // 2
    sibling = layer + 1 - 2 * (layer % 2)
    own = blocks // 2

    loads = [pltpu.make_async_copy(encw_hbm, encw, load_sem.at[0])]
    for b in range(own):
        span = pl.ds(b * rows, rows)
        loads.append(pltpu.make_async_copy(resid_hbm.at[span], resid.at[span], load_sem.at[1 + b]))
    for load in loads:
        load.start()
    dec_loads = [pltpu.make_async_copy(decw_hbm.at[s], decw.at[s], dec_sem.at[s]) for s in range(n_layer)]

    barrier = pltpu.get_barrier_semaphore()
    partner = (layer + half) % n_layer
    for where in ({"dp": 1 - dp}, {"layer": sibling}, {"layer": partner}):
        pl.semaphore_signal(barrier, inc=1, device_id=where, device_id_type=MESH)

    @pl.when(z > 0)
    def _():
        pl.semaphore_signal(barrier, inc=1, device_id={"feat": z - 1}, device_id_type=MESH)

    @pl.when(z < n_feat - 1)
    def _():
        pl.semaphore_signal(barrier, inc=1, device_id={"feat": z + 1}, device_id_type=MESH)

    ends = jnp.where(z == 0, 1, 0) + jnp.where(z == n_feat - 1, 1, 0)
    pl.semaphore_wait(barrier, 5 - ends)

    def block_of(i):
        return (dp if i < own else 1 - dp) * own + i % own

    def sent(source, i, sems, where):
        block = block_of(i)
        return pltpu.make_async_remote_copy(
            src_ref=acts.at[source, block],
            dst_ref=acts.at[source, block],
            send_sem=sems.at[i],
            recv_sem=acts_sem.at[source, block],
            device_id=where,
            device_id_type=MESH,
        )

    def dp_copy(i):
        return sent(layer, i, dp_send, {"dp": 1 - dp})

    def sib_copy(i):
        return sent(layer, i, sib_send, {"layer": sibling})

    def far_copy(i):
        return sent(layer, i, far_send, {"layer": partner})

    def relay_copy(i):
        return sent(partner, i, relay_send, {"layer": sibling})

    def arrived(source, i):
        sent(source, i, dp_send, {"dp": 1 - dp}).wait_recv()

    def spread(i):
        @pl.when(layer < half)
        def _():
            far_copy(i).start()

        @pl.when(layer % 2 == 0)
        def _():
            sib_copy(i).start()

    def encode(i):
        pre = jnp.dot(resid[i * rows : (i + 1) * rows], encw[...], preferred_element_type=jnp.float32)
        pre = jnp.maximum(pre + encb_ref[...], 0.0)
        for k in range(rows // SEQ):
            length = lengths_ref[i * (rows // SEQ) + k]
            piece = pre[k * SEQ : (k + 1) * SEQ]
            position = lax.broadcasted_iota(jnp.int32, piece.shape, 0)
            piece = jnp.where(position < length, piece, 0.0)
            acts[layer, block_of(i), pl.ds(k * SEQ, SEQ), :] = piece.astype(jnp.bfloat16)
        dp_copy(i).start()
        spread(i)

    def take(i):
        arrived(layer, i)
        spread(i)

    def relay(i):
        @pl.when(layer >= half)
        def _():
            arrived(layer - half, i)
            relay_copy(i).start()

    def z_copy(i, j, up):
        landing, sems = (from_low, low_sem) if up else (from_high, high_sem)
        return pltpu.make_async_remote_copy(
            src_ref=sbuf.at[i, j],
            dst_ref=landing.at[i, j],
            send_sem=z_send.at[i, j],
            recv_sem=sems.at[i, j],
            device_id={"feat": z + 1 if up else z - 1},
            device_id_type=MESH,
        )

    def decode(i):
        block = block_of(i)
        acc[...] = jnp.dot(acts[layer, block], decw[layer], preferred_element_type=jnp.float32)
        for s in range(n_layer - 1):

            @pl.when(s < layer)
            def _():
                @pl.when(s + half != layer)
                def _():
                    arrived(s, i)

                acc[...] += jnp.dot(acts[s, block], decw[s], preferred_element_type=jnp.float32)

        for j in range(n_feat):
            first = j * chunk
            part[i, j, 0:rows, :] = acc[:, first : first + main]
            tail = acc[:, first + main : first + chunk]
            part[i, j, rows : rows + tall, :] = jnp.concatenate(
                [tail[k * tall : (k + 1) * tall] for k in range(packs)], axis=1
            )

        @pl.when(z == 0)
        def _():
            for j in reversed(range(1, n_feat)):
                sbuf[i, j] = part[i, j].astype(jnp.bfloat16)
                z_copy(i, j, True).start()

        @pl.when(z == n_feat - 1)
        def _():
            for j in range(n_feat - 1):
                sbuf[i, j] = part[i, j].astype(jnp.bfloat16)
                z_copy(i, j, False).start()

    def forward(i, j, up):
        z_copy(i, j, up).wait_recv()
        landing = from_low if up else from_high
        sbuf[i, j] = (part[i, j] + landing[i, j].astype(jnp.float32)).astype(jnp.bfloat16)
        z_copy(i, j, up).start()

    def pass_on(i):
        for place in range(1, n_feat - 1):

            @pl.when(z == place)
            def _():
                ups = [(j, True) for j in reversed(range(place + 1, n_feat))]
                downs = [(j, False) for j in range(place)]
                order = ups + downs if len(ups) >= len(downs) else downs + ups
                for j, up in order:
                    forward(i, j, up)

    def finish(i):
        @pl.when(z > 0)
        def _():
            z_copy(i, z, True).wait_recv()
            part[i, z] += from_low[i, z].astype(jnp.float32)

        @pl.when(z < n_feat - 1)
        def _():
            z_copy(i, z, False).wait_recv()
            part[i, z] += from_high[i, z].astype(jnp.float32)

        span = pl.ds(pl.multiple_of(block_of(i) * rows, rows), rows)
        bias = decb_ref[...]
        total = part[i, z, 0:rows, :] + bias[:, 0:main]
        out_ref[0:main, span] = total.T.astype(jnp.bfloat16)
        tail = part[i, z, rows : rows + tall, :]
        tail = jnp.concatenate([tail[:, k * rem : (k + 1) * rem] for k in range(packs)], axis=0)
        tail = tail + bias[:, main:chunk]
        out_ref[main:chunk, span] = tail.T.astype(jnp.bfloat16)

    loads[0].wait()
    for i in range(own):
        loads[1 + i].wait()
        if i == 0:
            for load in dec_loads:
                load.start()
        encode(i)
    for i in range(blocks):
        relay(i)
        if 1 <= i <= own:
            take(own + i - 1)
        if i == 0:
            for load in dec_loads:
                load.wait()
        decode(i)
        if i >= 1:
            pass_on(i - 1)
        if i >= LAG:
            finish(i - LAG)
    pass_on(blocks - 1)
    for i in range(blocks - LAG, blocks):
        finish(i)

    for i in range(blocks):
        if i < own:
            dp_copy(i).wait_send()

        @pl.when(layer < half)
        def _():
            far_copy(i).wait_send()

        @pl.when(layer % 2 == 0)
        def _():
            sib_copy(i).wait_send()

        @pl.when(layer >= half)
        def _():
            relay_copy(i).wait_send()

        for j in range(n_feat):

            @pl.when(z != j)
            def _():
                z_copy(i, j, True).wait_send()


def with_kernel(n_feat, n_layer, resid, enc_weight, enc_bias, dec_weight, dec_bias, lengths):
    _, own_rows, width = resid.shape
    feats = enc_weight.shape[2]
    columns = dec_weight.shape[3]
    chunk = columns // n_feat
    main = chunk // LANES * LANES
    rem = chunk - main
    blocks = BLOCKS
    rows = 2 * own_rows // blocks
    tall = rows // (main // rem)
    packed = (blocks, n_feat, rows + tall, main)
    anywhere = pl.BlockSpec(memory_space=pl.ANY)
    vmem = pl.BlockSpec(memory_space=pltpu.VMEM)
    dma = pltpu.SemaphoreType.DMA
    out = pl.pallas_call(
        functools.partial(kernel, n_feat, n_layer, blocks, rows, main, rem),
        out_shape=jax.ShapeDtypeStruct((chunk, 2 * own_rows), jnp.bfloat16),
        in_specs=[pl.BlockSpec(memory_space=pltpu.SMEM), anywhere, anywhere, vmem, anywhere, vmem],
        out_specs=vmem,
        scratch_shapes=[
            pltpu.VMEM((own_rows, width), jnp.bfloat16),
            pltpu.VMEM((width, feats), jnp.bfloat16),
            pltpu.VMEM((n_layer, feats, columns), jnp.bfloat16),
            pltpu.VMEM((n_layer, blocks, rows, feats), jnp.bfloat16),
            pltpu.VMEM((rows, columns), jnp.float32),
            pltpu.VMEM(packed, jnp.float32),
            pltpu.VMEM(packed, jnp.bfloat16),
            pltpu.VMEM(packed, jnp.bfloat16),
            pltpu.VMEM(packed, jnp.bfloat16),
            dma((1 + blocks // 2,)),
            dma((n_layer,)),
            dma((n_layer, blocks)),
            dma((blocks,)),
            dma((blocks,)),
            dma((blocks,)),
            dma((blocks,)),
            dma((blocks, n_feat)),
            dma((blocks, n_feat)),
            dma((blocks, n_feat)),
        ],
        compiler_params=pltpu.CompilerParams(
            collective_id=0, has_side_effects=True, vmem_limit_bytes=56 * 2**20
        ),
    )(lengths, resid[0], enc_weight[0], enc_bias, dec_weight[0], dec_bias)
    return out.T[None]


def suits_kernel(sizes, resid, dec_weight):
    chunk = dec_weight.shape[3] // (sizes["dp"] * sizes["feat"])
    main, rem = chunk // LANES * LANES, chunk % LANES
    rows = resid.shape[1] // BLOCKS
    if sizes["dp"] != 2 or sizes["layer"] != 4 or sizes["feat"] < 2 or main == 0 or rem == 0:
        return False
    return main % rem == 0 and rows % SEQ == 0 and rows % (16 * (main // rem)) == 0


def solution(mesh):
    in_specs = (
        P("layer", "dp", None),
        P("layer", None, "feat"),
        P("layer", "feat"),
        P("layer", None, "feat", "dp"),
        P("layer", ("dp", "feat")),
        P("dp"),
    )
    out_specs = P("layer", None, ("dp", "feat"))
    sizes = dict(mesh.shape)

    def whole(resid, enc_weight, enc_bias, dec_weight, dec_bias, lengths):
        body = with_collectives
        if suits_kernel(sizes, resid, dec_weight):
            body = functools.partial(with_kernel, sizes["feat"], sizes["layer"])
        mapped = jax.shard_map(body, mesh=mesh, in_specs=in_specs, out_specs=out_specs, check_vma=False)
        return mapped(resid, enc_weight, enc_bias, dec_weight, dec_bias, lengths)

    return whole
```

```python
import functools

import jax
import jax.numpy as jnp
from jax import lax
from jax.experimental import pallas as pl
from jax.experimental.pallas import tpu as pltpu
from jax.sharding import PartitionSpec as P

SEQ = 128
LANES = 128
BLOCKS = 8
LAG = 3
MESH = pl.DeviceIdType.MESH


def passed_along(array, axis, by):
    size = lax.axis_size(axis)
    pairs = [(i, i + by) for i in range(size) if 0 <= i + by < size]
    return lax.ppermute(array, axis, pairs)


def with_collectives(resid, enc_weight, enc_bias, dec_weight, dec_bias, lengths):
    valid = (jnp.arange(SEQ)[None, :] < lengths[:, None]).reshape(-1).astype(jnp.float32)
    pre = jnp.dot(resid[0], enc_weight[0], preferred_element_type=jnp.float32) + enc_bias[0]
    acts = (jax.nn.relu(pre) * valid[:, None]).astype(jnp.bfloat16)
    target = lax.axis_index("layer")
    decoders = dec_weight[0]
    all_rows = lax.all_gather(acts, "dp", axis=0, tiled=True)
    initial = jnp.zeros((all_rows.shape[0], decoders.shape[2]), jnp.float32)
    pieces = [(all_rows, target)]
    current = all_rows
    for step in range(1, lax.axis_size("layer")):
        current = passed_along(current, "layer", 1)
        pieces.append((current, target - step))
    total = initial
    for block, source in pieces:

        def apply_dec(carry):
            matrix = lax.dynamic_index_in_dim(decoders, jnp.maximum(source, 0), 0, keepdims=False)
            return carry + jnp.dot(block, matrix, preferred_element_type=jnp.float32)

        total = lax.cond((source >= 0) & (source <= target), apply_dec, lambda carry: carry, total)
    summed = lax.psum_scatter(total, "feat", scatter_dimension=1, tiled=True)
    return (summed + dec_bias[0][None, :]).astype(jnp.bfloat16)[None]


def kernel(
    n_feat, n_layer, blocks, rows, main, rem,
    lengths_ref, resid_hbm, encw_hbm, encb_ref, decw_hbm, decb_ref,
    out_ref,
    resid, encw, decw, acts, acc, part, sbuf, from_low, from_high,
    load_sem, dec_sem, acts_sem, dp_send, sib_send, far_send, relay_send, z_send, low_sem, high_sem,
):
    dp, layer, z = lax.axis_index("dp"), lax.axis_index("layer"), lax.axis_index("feat")
    chunk = main + rem
    packs = main // rem
    tall = rows // packs
    half = n_layer // 2
    sibling = layer + 1 - 2 * (layer % 2)
    own = blocks // 2

    loads = [pltpu.make_async_copy(encw_hbm, encw, load_sem.at[0])]
    for b in range(own):
        span = pl.ds(b * rows, rows)
        loads.append(pltpu.make_async_copy(resid_hbm.at[span], resid.at[span], load_sem.at[1 + b]))
    for load in loads:
        load.start()
    dec_loads = [pltpu.make_async_copy(decw_hbm.at[s], decw.at[s], dec_sem.at[s]) for s in range(n_layer)]

    barrier = pltpu.get_barrier_semaphore()
    partner = (layer + half) % n_layer
    for where in ({"dp": 1 - dp}, {"layer": sibling}, {"layer": partner}):
        pl.semaphore_signal(barrier, inc=1, device_id=where, device_id_type=MESH)

    @pl.when(z > 0)
    def _():
        pl.semaphore_signal(barrier, inc=1, device_id={"feat": z - 1}, device_id_type=MESH)

    @pl.when(z < n_feat - 1)
    def _():
        pl.semaphore_signal(barrier, inc=1, device_id={"feat": z + 1}, device_id_type=MESH)

    ends = jnp.where(z == 0, 1, 0) + jnp.where(z == n_feat - 1, 1, 0)
    pl.semaphore_wait(barrier, 5 - ends)

    def block_of(i):
        return (dp if i < own else 1 - dp) * own + i % own

    def sent(source, i, sems, where):
        block = block_of(i)
        return pltpu.make_async_remote_copy(
            src_ref=acts.at[source, block],
            dst_ref=acts.at[source, block],
            send_sem=sems.at[i],
            recv_sem=acts_sem.at[source, block],
            device_id=where,
            device_id_type=MESH,
        )

    def dp_copy(i):
        return sent(layer, i, dp_send, {"dp": 1 - dp})

    def sib_copy(i):
        return sent(layer, i, sib_send, {"layer": sibling})

    def far_copy(i):
        return sent(layer, i, far_send, {"layer": partner})

    def relay_copy(i):
        return sent(partner, i, relay_send, {"layer": sibling})

    def arrived(source, i):
        sent(source, i, dp_send, {"dp": 1 - dp}).wait_recv()

    def spread(i):
        @pl.when(layer < half)
        def _():
            far_copy(i).start()

        @pl.when(layer % 2 == 0)
        def _():
            sib_copy(i).start()

    def encode(i):
        pre = jnp.dot(resid[i * rows : (i + 1) * rows], encw[...], preferred_element_type=jnp.float32)
        pre = jnp.maximum(pre + encb_ref[...], 0.0)
        for k in range(rows // SEQ):
            length = lengths_ref[i * (rows // SEQ) + k]
            piece = pre[k * SEQ : (k + 1) * SEQ]
            position = lax.broadcasted_iota(jnp.int32, piece.shape, 0)
            piece = jnp.where(position < length, piece, 0.0)
            acts[layer, block_of(i), pl.ds(k * SEQ, SEQ), :] = piece.astype(jnp.bfloat16)
        spread(i)
        dp_copy(i).start()

    def take(i):
        arrived(layer, i)
        spread(i)

    def relay(i):
        @pl.when(layer >= half)
        def _():
            arrived(layer - half, i)
            relay_copy(i).start()

    def z_copy(i, j, up):
        landing, sems = (from_low, low_sem) if up else (from_high, high_sem)
        return pltpu.make_async_remote_copy(
            src_ref=sbuf.at[i, j],
            dst_ref=landing.at[i, j],
            send_sem=z_send.at[i, j],
            recv_sem=sems.at[i, j],
            device_id={"feat": z + 1 if up else z - 1},
            device_id_type=MESH,
        )

    def ahead(i):
        if i + 1 < blocks:
            relay(i + 1)
        if i + 2 < own:
            loads[3 + i].wait()
            encode(i + 2)
        if i < own:
            take(own + i)

    def decode(i):
        block = block_of(i)
        acc[...] = jnp.dot(acts[layer, block], decw[layer], preferred_element_type=jnp.float32)
        for s in reversed(range(n_layer - 1)):
            if s == half - 1 and i == 0:
                relay(0)

            @pl.when(s < layer)
            def _():
                @pl.when(s + half != layer)
                def _():
                    arrived(s, i)

                acc[...] += jnp.dot(acts[s, block], decw[s], preferred_element_type=jnp.float32)

        ahead(i)
        for j in range(n_feat):
            first = j * chunk
            part[i, j, 0:rows, :] = acc[:, first : first + main]
            tail = acc[:, first + main : first + chunk]
            part[i, j, rows : rows + tall, :] = jnp.concatenate(
                [tail[k * tall : (k + 1) * tall] for k in range(packs)], axis=1
            )

        @pl.when(z == 0)
        def _():
            for j in reversed(range(1, n_feat)):
                sbuf[i, j] = part[i, j].astype(jnp.bfloat16)
                z_copy(i, j, True).start()

        @pl.when(z == n_feat - 1)
        def _():
            for j in range(n_feat - 1):
                sbuf[i, j] = part[i, j].astype(jnp.bfloat16)
                z_copy(i, j, False).start()

    def forward(i, j, up):
        z_copy(i, j, up).wait_recv()
        landing = from_low if up else from_high
        sbuf[i, j] = (part[i, j] + landing[i, j].astype(jnp.float32)).astype(jnp.bfloat16)
        z_copy(i, j, up).start()

    def pass_on(i):
        for place in range(1, n_feat - 1):

            @pl.when(z == place)
            def _():
                ups = [(j, True) for j in reversed(range(place + 1, n_feat))]
                downs = [(j, False) for j in range(place)]
                order = ups + downs if len(ups) >= len(downs) else downs + ups
                for j, up in order:
                    forward(i, j, up)

    def finish(i):
        @pl.when(z > 0)
        def _():
            z_copy(i, z, True).wait_recv()
            part[i, z] += from_low[i, z].astype(jnp.float32)

        @pl.when(z < n_feat - 1)
        def _():
            z_copy(i, z, False).wait_recv()
            part[i, z] += from_high[i, z].astype(jnp.float32)

        span = pl.ds(pl.multiple_of(block_of(i) * rows, rows), rows)
        bias = decb_ref[...]
        total = part[i, z, 0:rows, :] + bias[:, 0:main]
        out_ref[0:main, span] = total.T.astype(jnp.bfloat16)
        tail = part[i, z, rows : rows + tall, :]
        tail = jnp.concatenate([tail[:, k * rem : (k + 1) * rem] for k in range(packs)], axis=0)
        tail = tail + bias[:, main:chunk]
        out_ref[main:chunk, span] = tail.T.astype(jnp.bfloat16)

    loads[0].wait()
    loads[1].wait()
    for load in dec_loads:
        load.start()
    encode(0)
    loads[2].wait()
    encode(1)
    for load in dec_loads:
        load.wait()
    for i in range(blocks):
        decode(i)
        if i >= 1:
            pass_on(i - 1)
        if i >= LAG:
            finish(i - LAG)
    pass_on(blocks - 1)
    for i in range(blocks - LAG, blocks):
        finish(i)

    for i in range(blocks):
        if i < own:
            dp_copy(i).wait_send()

        @pl.when(layer < half)
        def _():
            far_copy(i).wait_send()

        @pl.when(layer % 2 == 0)
        def _():
            sib_copy(i).wait_send()

        @pl.when(layer >= half)
        def _():
            relay_copy(i).wait_send()

        for j in range(n_feat):

            @pl.when(z != j)
            def _():
                z_copy(i, j, True).wait_send()


def with_kernel(n_feat, n_layer, resid, enc_weight, enc_bias, dec_weight, dec_bias, lengths):
    _, own_rows, width = resid.shape
    feats = enc_weight.shape[2]
    columns = dec_weight.shape[3]
    chunk = columns // n_feat
    main = chunk // LANES * LANES
    rem = chunk - main
    blocks = BLOCKS
    rows = 2 * own_rows // blocks
    tall = rows // (main // rem)
    packed = (blocks, n_feat, rows + tall, main)
    anywhere = pl.BlockSpec(memory_space=pl.ANY)
    vmem = pl.BlockSpec(memory_space=pltpu.VMEM)
    dma = pltpu.SemaphoreType.DMA
    out = pl.pallas_call(
        functools.partial(kernel, n_feat, n_layer, blocks, rows, main, rem),
        out_shape=jax.ShapeDtypeStruct((chunk, 2 * own_rows), jnp.bfloat16),
        in_specs=[pl.BlockSpec(memory_space=pltpu.SMEM), anywhere, anywhere, vmem, anywhere, vmem],
        out_specs=vmem,
        scratch_shapes=[
            pltpu.VMEM((own_rows, width), jnp.bfloat16),
            pltpu.VMEM((width, feats), jnp.bfloat16),
            pltpu.VMEM((n_layer, feats, columns), jnp.bfloat16),
            pltpu.VMEM((n_layer, blocks, rows, feats), jnp.bfloat16),
            pltpu.VMEM((rows, columns), jnp.float32),
            pltpu.VMEM(packed, jnp.float32),
            pltpu.VMEM(packed, jnp.bfloat16),
            pltpu.VMEM(packed, jnp.bfloat16),
            pltpu.VMEM(packed, jnp.bfloat16),
            dma((1 + blocks // 2,)),
            dma((n_layer,)),
            dma((n_layer, blocks)),
            dma((blocks,)),
            dma((blocks,)),
            dma((blocks,)),
            dma((blocks,)),
            dma((blocks, n_feat)),
            dma((blocks, n_feat)),
            dma((blocks, n_feat)),
        ],
        compiler_params=pltpu.CompilerParams(
            collective_id=0, has_side_effects=True, vmem_limit_bytes=56 * 2**20
        ),
    )(lengths, resid[0], enc_weight[0], enc_bias, dec_weight[0], dec_bias)
    return out.T[None]


def suits_kernel(sizes, resid, dec_weight):
    chunk = dec_weight.shape[3] // (sizes["dp"] * sizes["feat"])
    main, rem = chunk // LANES * LANES, chunk % LANES
    rows = resid.shape[1] // BLOCKS
    if sizes["dp"] != 2 or sizes["layer"] != 4 or sizes["feat"] < 2 or main == 0 or rem == 0:
        return False
    return main % rem == 0 and rows % SEQ == 0 and rows % (16 * (main // rem)) == 0


def solution(mesh):
    in_specs = (
        P("layer", "dp", None),
        P("layer", None, "feat"),
        P("layer", "feat"),
        P("layer", None, "feat", "dp"),
        P("layer", ("dp", "feat")),
        P("dp"),
    )
    out_specs = P("layer", None, ("dp", "feat"))
    sizes = dict(mesh.shape)

    def whole(resid, enc_weight, enc_bias, dec_weight, dec_bias, lengths):
        body = with_collectives
        if suits_kernel(sizes, resid, dec_weight):
            body = functools.partial(with_kernel, sizes["feat"], sizes["layer"])
        mapped = jax.shard_map(body, mesh=mesh, in_specs=in_specs, out_specs=out_specs, check_vma=False)
        return mapped(resid, enc_weight, enc_bias, dec_weight, dec_bias, lengths)

    return whole
```
